32 devices in a mesh: groups: 2 (over y), band: 4 (over z), sector: 2 (over x), chan: 2 (over core).
Axes of the slice: x: 2, y: 2, z: 4, core: 2. Of those that a mesh axis runs over, the one named last changes fastest.
Arguments:
- grid_inputs: bfloat16 [8, 2, 2048, 227], P(('groups', 'band'), 'sector'), parts along dimension 0, may hold values from -6 to 6
- mesh_node_embedding: bfloat16 [8, 2, 256, 512], P(('groups', 'band'), 'sector', None, 'chan'), parts along dimension 0, may hold values from -6 to 6
- enc_counts: int32 [4, 2, 4], P('band', 'sector'), may hold values from 1 to 4, as said below
- enc_source: int32 [4, 2, 8], P('band', 'sector'), may hold values from 0 to 15
- enc_target: int32 [4, 2, 8], P('band', 'sector'), may hold values from 0 to 1
- enc_blocks: bfloat16 [4, 2, 8, 128, 128], P('band', 'sector'), may hold values from -0.25 to 0.25
- proc_source: int32 [4, 2, 8], P('band', 'sector'), may hold values from 0 to 3, as said below
- proc_target: int32 [4, 2, 8], P('band', 'sector'), may hold values from 0 to 1
- proc_blocks: bfloat16 [4, 2, 8, 128, 128], P('band', 'sector'), may hold values from -0.25 to 0.25
- bound_blocks: int32 [4, 2, 2, 1], P('band', 'sector'), may hold values from 0 to 1
- dec_blocks: bfloat16 [4, 2, 8, 128, 128], P('band', 'sector'), may hold values from -0.5 to 0.5
- grid_w1: bfloat16 [227, 512], P(None, 'chan'), may hold values from -0.375 to 0.375
- grid_gain: float32 [512], replicated, may hold values from 0.1 to 1.9
- grid_w2: bfloat16 [512, 512], P(None, 'chan'), may hold values from -0.25 to 0.25
- enc_w1: bfloat16 [2, 512, 512], P(None, None, 'chan'), may hold values from -0.1875 to 0.1875
- enc_gain: float32 [512], replicated, may hold values from 0.1 to 1.9
- enc_w2: bfloat16 [512, 512], P(None, 'chan'), may hold values from -0.25 to 0.25
- proc_w1: bfloat16 [2, 512, 512], P(None, None, 'chan'), may hold values from -0.1875 to 0.1875
- proc_gain: float32 [512], replicated, may hold values from 0.1 to 1.9
- processor_second_weight: bfloat16 [512, 512], P(None, 'chan'), may hold values from -0.25 to 0.25
- dec_w1: bfloat16 [2, 512, 512], P(None, None, 'chan'), may hold values from -0.1875 to 0.1875
- dec_gain: float32 [512], replicated, may hold values from 0.1 to 1.9
- dec_w2: bfloat16 [512, 227], replicated, may hold values from -0.25 to 0.25
Outputs:
- prediction: float32 [8, 2, 2048, 227], P(('groups', 'band'), 'sector'), parts along dimension 0
The draws below stay inside these ranges and needn't reach their ends.
There are 2 independent parts, one for each index of `groups`. The reference program is written for one: setup_inputs(seed, part) draws one part's arguments, and reference() takes and returns one part's arrays. A program takes and returns all parts, laid end to end along the dimension named above; an argument that names none is the same for every part. Nothing has to cross between parts.
Inputs may be any that keep to these rules, and one draw needn't show every extreme that they name: `enc_counts`: for each band and sector, its 8 encoder edge blocks are ordered by receiving band; each band receives 1 to 4 of them, they sum to 8, and in each sector one band receives exactly 4 from every band. `proc_source`: values below 2 are own blocks, then 1 from the previous sector, then 1 from the next; edge block k < 2 reads source 2 + k.
All inputs are finite; a program needn't handle non-finite values.
Results may differ from the reference program's by a relative error of at most 0.011.
Values may be sent and summed in bfloat16 or wider, within the bound.
A program may use at most 64 MiB of HBM per device.

```python
import jax
import jax.numpy as jnp
from jax import lax

LAT = 512
CH = 227
BLK = 128
G_BLK = 16
M_BLK = 2
CAP = 4
P_BLK = 8
BND = 1
BANDS = 4
SECTORS = 2
G_DEV = 2048
M_DEV = 256
E_BLK = 8


def draw_enc_counts(key, part):
    key = jax.random.fold_in(key, 11)
    busy_key, fill_key = jax.random.split(key)
    busiest = jax.random.randint(busy_key, (SECTORS,), 0, BANDS)
    peer_ids = jnp.arange(BANDS, dtype=jnp.int32)
    counts = jnp.ones((BANDS, SECTORS, BANDS), jnp.int32)
    counts = counts + (CAP - 1) * (peer_ids[None, None, :] == busiest[None, :, None]).astype(jnp.int32)

    def add_unit(position, current):
        scores = jax.random.randint(jax.random.fold_in(fill_key, position), current.shape, 0, 1 << 20) * BANDS + peer_ids
        scores = jnp.where(current < CAP, scores, -1)
        chosen = jnp.argmax(scores, axis=-1)
        return current + (peer_ids == chosen[..., None]).astype(jnp.int32)
    return lax.fori_loop(0, E_BLK - BANDS - CAP + 1, add_unit, counts).astype(jnp.int32)


def draw_proc_source(key, part):
    key = jax.random.fold_in(key, 23)
    random_part = jax.random.randint(key, (BANDS, SECTORS, P_BLK), 0, M_BLK + 2 * BND)
    position = jnp.arange(P_BLK, dtype=jnp.int32)[None, None, :]
    return jnp.where(position < 2 * BND, M_BLK + position, random_part).astype(jnp.int32)


def plant(entries, rng, least, largest):
    longest = entries.shape.index(max(entries.shape))
    spots = []
    for shift in (0, 1):
        where = [jax.random.randint(jax.random.fold_in(rng, axis), (), 0, length) for axis, length in enumerate(entries.shape)]
        where[longest] = (where[longest] + shift) % entries.shape[longest]
        spots.append(tuple(where))
    return entries.at[spots[0]].set(least).at[spots[1]].set(largest)


def shard_levels(key, shape, cuts, smallest, high):
    level = 1.0
    for dim, shards_of in cuts:
        heights = jax.random.uniform(jax.random.fold_in(jax.random.fold_in(key, 6), dim), (shards_of,), jnp.float32, smallest / len(cuts), high / len(cuts))
        level = level * jnp.repeat(jnp.exp(heights), shape[dim] // shards_of).reshape((-1,) + (1,) * (len(shape) - 1 - dim))
    return level


def centred(stream_key, extent, scale, reach, pieces=(), kind=jnp.bfloat16):
    drawn = scale * jax.random.normal(stream_key, extent, jnp.float32)
    if pieces:
        drawn = drawn * shard_levels(stream_key, extent, pieces, -0.22, 0.18)
    return jnp.clip(drawn, -reach, reach).astype(kind)


def setup_inputs(seed: int = 0, part: int = 0) -> dict:
    arg_keys = jax.random.split(jax.random.key(seed), 24)
    part_keys = jax.random.split(jax.random.fold_in(arg_keys[23], part), 24)
    grid_inputs = centred(part_keys[0], (BANDS, SECTORS, G_DEV, CH), 1.0, 6.0, ((0, 4), (1, 2)))
    mesh_node_embedding = centred(part_keys[1], (BANDS, SECTORS, M_DEV, LAT), 1.0, 6.0, ((0, 4), (1, 2), (3, 2)))
    enc_counts = draw_enc_counts(jax.random.fold_in(arg_keys[23], 71), part)
    enc_source = plant(jax.random.randint(arg_keys[3], (BANDS, SECTORS, E_BLK), 0, G_BLK), jax.random.fold_in(arg_keys[3], 1), 0, G_BLK - 1).astype(jnp.int32)
    enc_target = plant(jax.random.randint(arg_keys[4], (BANDS, SECTORS, E_BLK), 0, M_BLK), jax.random.fold_in(arg_keys[4], 1), 0, M_BLK - 1).astype(jnp.int32)
    enc_blocks = centred(arg_keys[5], (BANDS, SECTORS, E_BLK, BLK, BLK), (BLK * E_BLK // M_BLK) ** -0.5, 0.25, ((0, 4), (1, 2)))
    proc_source = draw_proc_source(jax.random.fold_in(arg_keys[23], 71), part)
    proc_target = plant(jax.random.randint(arg_keys[7], (BANDS, SECTORS, P_BLK), 0, M_BLK), jax.random.fold_in(arg_keys[7], 1), 0, M_BLK - 1).astype(jnp.int32)
    proc_blocks = centred(arg_keys[8], (BANDS, SECTORS, P_BLK, BLK, BLK), (BLK * P_BLK // M_BLK) ** -0.5, 0.25, ((0, 4), (1, 2)))
    bound_blocks = plant(jax.random.randint(arg_keys[9], (BANDS, SECTORS, 2, BND), 0, M_BLK), jax.random.fold_in(arg_keys[9], 1), 0, M_BLK - 1).astype(jnp.int32)
    dec_blocks = centred(arg_keys[10], (BANDS, SECTORS, E_BLK, BLK, BLK), (BLK * max(1, E_BLK // G_BLK)) ** -0.5, 0.5, ((0, 4), (1, 2)))
    grid_w1 = centred(arg_keys[11], (CH, LAT), CH ** -0.5, 0.375, ((1, 2),))
    grid_gain = jnp.clip(1.0 + 0.18 * jax.random.normal(arg_keys[12], (LAT,), jnp.float32), 0.1, 1.9)
    grid_w2 = centred(arg_keys[13], (LAT, LAT), LAT ** -0.5, 0.25, ((1, 2),))
    enc_w1 = centred(arg_keys[14], (2, LAT, LAT), (2 * LAT) ** -0.5, 0.1875, ((2, 2),))
    enc_gain = jnp.clip(1.0 + 0.18 * jax.random.normal(arg_keys[15], (LAT,), jnp.float32), 0.1, 1.9)
    enc_w2 = centred(arg_keys[16], (LAT, LAT), LAT ** -0.5, 0.25, ((1, 2),))
    proc_w1 = centred(arg_keys[17], (2, LAT, LAT), (2 * LAT) ** -0.5, 0.1875, ((2, 2),))
    proc_gain = jnp.clip(1.0 + 0.18 * jax.random.normal(arg_keys[18], (LAT,), jnp.float32), 0.1, 1.9)
    processor_second_weight = centred(arg_keys[19], (LAT, LAT), LAT ** -0.5, 0.25, ((1, 2),))
    dec_w1 = centred(arg_keys[20], (2, LAT, LAT), (2 * LAT) ** -0.5, 0.1875, ((2, 2),))
    dec_gain = jnp.clip(1.0 + 0.18 * jax.random.normal(arg_keys[21], (LAT,), jnp.float32), 0.1, 1.9)
    dec_w2 = centred(arg_keys[22], (LAT, CH), LAT ** -0.5, 0.25)
    return {"grid_inputs": grid_inputs, "mesh_node_embedding": mesh_node_embedding, "enc_counts": enc_counts, "enc_source": enc_source, "enc_target": enc_target, "enc_blocks": enc_blocks, "proc_source": proc_source, "proc_target": proc_target, "proc_blocks": proc_blocks, "bound_blocks": bound_blocks, "dec_blocks": dec_blocks, "grid_w1": grid_w1, "grid_gain": grid_gain, "grid_w2": grid_w2, "enc_w1": enc_w1, "enc_gain": enc_gain, "enc_w2": enc_w2, "proc_w1": proc_w1, "proc_gain": proc_gain, "processor_second_weight": processor_second_weight, "dec_w1": dec_w1, "dec_gain": dec_gain, "dec_w2": dec_w2}


def matmul(left, right):
    return jnp.dot(left, right, preferred_element_type=jnp.float32)

def norm_silu(pre_act, gain):
    values = pre_act.astype(jnp.float32)
    center = values - lax.optimization_barrier(jnp.mean(values, axis=-1, keepdims=True))
    spread = lax.optimization_barrier(jnp.mean(center * center, axis=-1, keepdims=True))
    return jax.nn.silu(center * lax.rsqrt(spread + 1e-05) * gain.astype(jnp.float32)).astype(jnp.bfloat16)

def mesh_update(state, summed, w_in, gain, w_out):
    pre_act = (matmul(state, w_in[0]) + matmul(summed, w_in[1])).astype(jnp.bfloat16)
    return (state.astype(jnp.float32) + matmul(norm_silu(pre_act, gain), w_out)).astype(jnp.bfloat16)

def edge_products(blocks, rows):

    def per_band(pair):
        weights, inputs = pair
        return jnp.einsum('seij,sejf->seif', weights.astype(jnp.float32), inputs.astype(jnp.float32)).astype(jnp.bfloat16)
    return lax.map(per_band, (blocks, rows))

def source_sums(pair):
    hot, message = pair
    return jnp.einsum('seq,seif->sqif', hot, message.astype(jnp.float32)).astype(jnp.bfloat16)

def reference(grid_inputs, mesh_node_embedding, enc_counts, enc_source, enc_target, enc_blocks, proc_source, proc_target, proc_blocks, bound_blocks, dec_blocks, grid_w1, grid_gain, grid_w2, enc_w1, enc_gain, enc_w2, proc_w1, proc_gain, processor_second_weight, dec_w1, dec_gain, dec_w2):
    grid_pre = matmul(grid_inputs.reshape(-1, CH), grid_w1).astype(jnp.bfloat16)
    grid_latent = matmul(norm_silu(grid_pre, grid_gain), grid_w2).astype(jnp.bfloat16)
    device_ids = jnp.arange(BANDS * SECTORS, dtype=jnp.int32).reshape(BANDS, SECTORS, 1)
    grid_index = (device_ids * G_BLK + enc_source).astype(jnp.int32)
    chosen = jnp.take(grid_latent.reshape(-1, BLK, LAT), grid_index.reshape(-1), axis=0).reshape(BANDS, SECTORS, E_BLK, BLK, LAT)
    enc_message = edge_products(enc_blocks, chosen)
    count_ends = jnp.cumsum(enc_counts, axis=-1).astype(jnp.int32)
    edge_ids = jnp.arange(E_BLK, dtype=jnp.int32)
    peer_of = lax.optimization_barrier(jnp.sum((count_ends[:, :, None, :] <= edge_ids[None, None, :, None]).astype(jnp.int32), axis=-1)).astype(jnp.int32)
    sector_ids = jnp.arange(SECTORS, dtype=jnp.int32)[None, :, None]
    target_index = ((peer_of * SECTORS + sector_ids) * M_BLK + enc_target).astype(jnp.int32)
    pair_index = (peer_of * M_BLK + enc_target).astype(jnp.int32)
    pair_hot = (pair_index[..., None] == jnp.arange(BANDS * M_BLK, dtype=jnp.int32)).astype(jnp.float32)
    enc_part = lax.map(source_sums, (pair_hot, enc_message))
    enc_total = lax.optimization_barrier(jnp.sum(enc_part.astype(jnp.float32), axis=0)).reshape(SECTORS, BANDS, M_BLK, BLK, LAT)
    enc_sum = jnp.transpose(enc_total, (1, 0, 2, 3, 4)).astype(jnp.bfloat16)
    mesh_one = mesh_update(mesh_node_embedding.reshape(-1, LAT), enc_sum.reshape(-1, LAT), enc_w1, enc_gain, enc_w2)
    mesh_blocks = mesh_one.reshape(BANDS, SECTORS, M_BLK, BLK, LAT)
    list_index = (device_ids * M_BLK + bound_blocks.reshape(BANDS, SECTORS, 2 * BND)).astype(jnp.int32)
    listed = jnp.take(mesh_one.reshape(-1, BLK, LAT), list_index.reshape(-1), axis=0).reshape(BANDS, SECTORS, 2 * BND, BLK, LAT)
    from_prev = jnp.roll(listed[:, :, BND:], 1, axis=1)
    from_next = jnp.roll(listed[:, :, :BND], -1, axis=1)
    proc_sources = jnp.concatenate([mesh_blocks, from_prev, from_next], axis=2)
    source_count = M_BLK + 2 * BND
    proc_index = (device_ids * source_count + proc_source).astype(jnp.int32)
    proc_rows = jnp.take(proc_sources.reshape(-1, BLK, LAT), proc_index.reshape(-1), axis=0).reshape(BANDS, SECTORS, P_BLK, BLK, LAT)
    processor_edge_message = edge_products(proc_blocks, proc_rows)
    processor_onehot = (proc_target[..., None] == jnp.arange(M_BLK, dtype=jnp.int32)).astype(jnp.float32)
    processor_edge_sum = jnp.einsum('bsed,bseif->bsdif', processor_onehot, processor_edge_message.astype(jnp.float32)).astype(jnp.bfloat16)
    mesh_two = mesh_update(mesh_one, processor_edge_sum.reshape(-1, LAT), proc_w1, proc_gain, processor_second_weight)
    dec_rows = jnp.take(mesh_two.reshape(-1, BLK, LAT), target_index.reshape(-1), axis=0).reshape(BANDS, SECTORS, E_BLK, BLK, LAT)
    dec_message = edge_products(dec_blocks, dec_rows)
    grid_hot = (enc_source[..., None] == jnp.arange(G_BLK, dtype=jnp.int32)).astype(jnp.float32)
    dec_sum = jnp.einsum('bseg,bseif->bsgif', grid_hot, dec_message.astype(jnp.float32)).astype(jnp.bfloat16)
    dec_pre = (matmul(grid_latent, dec_w1[0]) + matmul(dec_sum.reshape(-1, LAT), dec_w1[1])).astype(jnp.bfloat16)
    prediction = matmul(norm_silu(dec_pre, dec_gain), dec_w2)
    return prediction.reshape(BANDS, SECTORS, G_DEV, CH)
```

```python
import functools

import jax
import jax.numpy as jnp
from jax import lax
from jax.experimental import pallas as pl
from jax.experimental.pallas import tpu as pltpu
from jax.sharding import PartitionSpec as P

MESH = pl.DeviceIdType.MESH
F32 = jnp.float32
BF16 = jnp.bfloat16
M_BLK = 2


def mm(a, b):
    return jnp.dot(a, b, preferred_element_type=F32)


def norm_silu(v, gain):
    n = 1.0 / v.shape[-1]
    center = v - jnp.sum(v, axis=-1, keepdims=True) * n
    spread = jnp.sum(center * center, axis=-1, keepdims=True) * n
    half = center * lax.rsqrt(spread + 1e-5) * (0.5 * gain)
    return (half + half * jnp.tanh(half)).astype(BF16)


def front_kernel(
    B, S, E, PE,
    counts, esrc, etgt, psrc, ptgt, bound,
    x, eblk, pblk, ggain, egain, pgain,
    emb, gw1, gw2, ew1, ew2, pw1, pw2, dw1,
    base, mall, dsum_w,
    emb_f, gw1_f, gw2_f, ew1_f, ew2_f, pw1_f, pw2_f, dw1_f,
    lat, xs, own, psend, precv, half_send, half_recv, m1, bsend, srcs, wide,
    loc_sem, wsend_sem, wrecv_sem, as_sem, ar_sem, hs_sem, hr_sem, bs_sem, br_sem,
    gs_sem, gr_sem, fs_sem, fr_sem,
):
    me = lax.axis_index("band")
    sec = lax.axis_index("sector")
    c = lax.axis_index("chan")
    oc = 1 - c
    hw = gw2.shape[-1]
    nxt = lax.rem(sec + 1, S)
    prv = lax.rem(sec + S - 1, S)
    mrows = emb.shape[0]
    rows = mrows // M_BLK
    g_blk = lat.shape[1]
    cols = pl.ds(pl.multiple_of(c * hw, hw), hw)
    ocols = pl.ds(pl.multiple_of(oc * hw, hw), hw)

    parts = [
        (gw1, gw1_f.at[:, cols]),
        (gw2, gw2_f.at[:, cols]),
        (emb, emb_f.at[:, cols]),
        (ew1, ew1_f.at[:, :, cols]),
        (dw1.at[0], dw1_f.at[:, cols]),
        (ew2, ew2_f.at[:, cols]),
        (pw1, pw1_f.at[:, :, cols]),
        (pw2, pw2_f.at[:, cols]),
        (dw1.at[1], dsum_w.at[:, cols]),
    ]
    local = [pltpu.make_async_copy(s, d, loc_sem.at[i]) for i, (s, d) in enumerate(parts)]
    for cp in local:
        cp.start()

    barrier = pltpu.get_barrier_semaphore()
    pl.semaphore_signal(barrier, inc=1, device_id={"chan": oc}, device_id_type=MESH)
    pl.semaphore_signal(barrier, inc=1, device_id={"sector": nxt}, device_id_type=MESH)
    pl.semaphore_signal(barrier, inc=1, device_id={"sector": prv}, device_id_type=MESH)
    for d in range(1, B):
        pl.semaphore_signal(
            barrier, inc=1, device_id={"band": lax.rem(me + d, B)}, device_id_type=MESH
        )
    pl.semaphore_wait(barrier, B + 2)

    remote = [
        pltpu.make_async_remote_copy(
            s, d, wsend_sem.at[i], wrecv_sem.at[i], device_id={"chan": oc}, device_id_type=MESH
        )
        for i, (s, d) in enumerate(parts)
    ]
    for cp in remote:
        cp.start()

    def arrived(i):
        local[i].wait()
        remote[i].wait_recv()

    arrived(0)
    arrived(1)

    chunk = 2 * rows

    def grid_step(i, _):
        r = pl.ds(pl.multiple_of(i * chunk, chunk), chunk)
        h = norm_silu(mm(x[r, :], gw1_f[...]), ggain[...])
        latent = mm(h, gw2_f[...]).astype(BF16)
        for k in range(2):
            for j in range(2):
                lat[k, 2 * i + j] = latent[j * rows : (j + 1) * rows, k * hw : (k + 1) * hw]
        return 0

    lax.fori_loop(0, g_blk // 2, grid_step, 0, unroll=2)

    for e in range(E):
        xs[e * rows : (e + 1) * rows, :] = lat[c, esrc[e]]

    def part_for(q):
        lo = jnp.int32(0)
        size = jnp.int32(0)
        for p in range(B):
            lo = lo + jnp.where(p < q, counts[p], 0)
            size = size + jnp.where(p == q, counts[p], 0)
        acc = []
        for m in range(M_BLK):
            pieces = []
            for e in range(E):
                keep = jnp.where((lo <= e) & (e < lo + size) & (etgt[e] == m), 1.0, 0.0)
                pieces.append(eblk[e] * keep.astype(BF16))
            acc.append(mm(jnp.concatenate(pieces, axis=1), xs[...]))
        return acc

    def band_copy(d):
        return pltpu.make_async_remote_copy(
            psend.at[d - 1], precv.at[d - 1], as_sem.at[d - 1], ar_sem.at[d - 1],
            device_id={"band": lax.rem(me + d, B)}, device_id_type=MESH,
        )

    def send_step(d, _):
        acc = part_for(lax.rem(me + d, B))
        for m in range(M_BLK):
            psend[d - 1, m * rows : (m + 1) * rows, :] = acc[m].astype(BF16)
        band_copy(d).start()
        return 0

    lax.fori_loop(1, B, send_step, 0, unroll=B <= 4)
    acc = part_for(me)
    for m in range(M_BLK):
        own[m * rows : (m + 1) * rows, :] = acc[m]

    arrived(2)
    arrived(3)
    wide[...] = mm(emb_f[...], ew1_f[0])
    arrived(4)

    def base_step(i, _):
        left = jnp.concatenate([lat[0, 2 * i], lat[0, 2 * i + 1]], axis=0)
        right = jnp.concatenate([lat[1, 2 * i], lat[1, 2 * i + 1]], axis=0)
        out = mm(left, dw1_f[:hw, :]) + mm(right, dw1_f[hw:, :])
        base[pl.ds(pl.multiple_of(i * chunk, chunk), chunk), :] = out.astype(BF16)
        return 0

    lax.fori_loop(0, g_blk // 2, base_step, 0)

    def take_step(d, _):
        band_copy(d).wait_recv()
        own[...] += precv[d - 1].astype(F32)
        return 0

    lax.fori_loop(1, B, take_step, 0, unroll=B <= 4)

    def update(k, summed, w1, gain, w2):
        half_send[k] = summed.astype(BF16)
        cp = pltpu.make_async_remote_copy(
            half_send.at[k], half_recv.at[k], hs_sem.at[k], hr_sem.at[k],
            device_id={"chan": oc}, device_id_type=MESH,
        )
        cp.start()
        pre = wide[...] + mm(half_send[k], w1[1, cols, :])
        cp.wait_recv()
        pre = pre + mm(half_recv[k], w1[1, ocols, :])
        cp.wait_send()
        return mm(norm_silu(pre, gain[...]), w2[...])

    arrived(5)
    one = (emb_f[...].astype(F32) + update(0, own[...], ew1_f, egain, ew2_f)).astype(BF16)
    for k in range(2):
        for j in range(M_BLK):
            m1[k, j] = one[j * rows : (j + 1) * rows, k * hw : (k + 1) * hw]
    bsend[0] = m1[c, bound[0]]
    bsend[1] = m1[c, bound[1]]
    to_next = pltpu.make_async_remote_copy(
        bsend.at[1], srcs.at[M_BLK], bs_sem.at[1], br_sem.at[0],
        device_id={"sector": nxt}, device_id_type=MESH,
    )
    to_prev = pltpu.make_async_remote_copy(
        bsend.at[0], srcs.at[M_BLK + 1], bs_sem.at[0], br_sem.at[1],
        device_id={"sector": prv}, device_id_type=MESH,
    )
    to_next.start()
    to_prev.start()
    for j in range(M_BLK):
        srcs[j] = m1[c, j]
    arrived(6)
    wide[...] = mm(one, pw1_f[0])
    to_next.wait_recv()
    to_prev.wait_recv()
    ys = jnp.concatenate([srcs[psrc[e]] for e in range(PE)], axis=0)
    for m in range(M_BLK):
        pieces = []
        for e in range(PE):
            keep = jnp.where(ptgt[e] == m, 1.0, 0.0)
            pieces.append(pblk[e] * keep.astype(BF16))
        own[m * rows : (m + 1) * rows, :] = mm(jnp.concatenate(pieces, axis=1), ys)
    arrived(7)
    two = (one.astype(F32) + update(1, own[...], pw1_f, pgain, pw2_f)).astype(BF16)
    for k in range(2):
        mall[k, me] = two[:, k * hw : (k + 1) * hw]

    def out_copy(d):
        return pltpu.make_async_remote_copy(
            mall.at[c, me], mall.at[c, me], gs_sem.at[d - 1], gr_sem.at[d - 1],
            device_id={"band": lax.rem(me + d, B)}, device_id_type=MESH,
        )

    def in_copy(d):
        src = lax.rem(me - d + B, B)
        return pltpu.make_async_remote_copy(
            mall.at[c, src], mall.at[c, src], gs_sem.at[d - 1], gr_sem.at[d - 1],
            device_id={"band": lax.rem(me + d, B)}, device_id_type=MESH,
        )

    def forward(d, half):
        src = lax.rem(me - d + B, B)
        return pltpu.make_async_remote_copy(
            mall.at[half, src], mall.at[half, src], fs_sem.at[d - 1], fr_sem.at[d - 1],
            device_id={"chan": oc}, device_id_type=MESH,
        )

    def gather_start(d, _):
        out_copy(d).start()
        return 0

    def gather_pass(d, _):
        in_copy(d).wait_recv()
        forward(d, c).start()
        return 0

    def gather_end(d, _):
        forward(d, oc).wait_recv()
        forward(d, c).wait_send()
        out_copy(d).wait_send()
        band_copy(d).wait_send()
        return 0

    lax.fori_loop(1, B, gather_start, 0, unroll=B <= 4)
    arrived(8)
    to_next.wait_send()
    to_prev.wait_send()
    for cp in remote:
        cp.wait_send()
    lax.fori_loop(1, B, gather_pass, 0, unroll=B <= 4)
    lax.fori_loop(1, B, gather_end, 0, unroll=B <= 4)


def back_kernel(B, E, counts, esrc, etgt, base, mall, dsum_w, dblk, dgain, dw2, out, acc):
    rows = dblk.shape[1]
    g_blk = acc.shape[0]
    hw = mall.shape[-1]
    for g in range(g_blk):
        acc[g] = base[g * rows : (g + 1) * rows, :].astype(F32)

    def edge(e, _):
        peer = jnp.int32(0)
        end = jnp.int32(0)
        for p in range(B):
            end = end + counts[p]
            peer = peer + jnp.where(end <= e, 1, 0)
        r = pl.ds(pl.multiple_of(etgt[e] * rows, rows), rows)
        add = jnp.zeros((rows, 2 * hw), F32)
        for k in range(2):
            msg = mm(dblk[e], mall[k, peer, r, :]).astype(BF16)
            add = add + mm(msg, dsum_w[k * hw : (k + 1) * hw, :])
        acc[esrc[e]] += add
        return 0

    lax.fori_loop(0, E, edge, 0, unroll=4)

    def final(i, _):
        v = jnp.concatenate([acc[2 * i], acc[2 * i + 1]], axis=0)
        h = norm_silu(v, dgain[...])
        out[pl.ds(pl.multiple_of(i * 2 * rows, 2 * rows), 2 * rows), :] = mm(h, dw2[...])
        return 0

    lax.fori_loop(0, g_blk // 2, final, 0, unroll=2)


def local(
    grid_inputs, emb, counts, esrc, etgt, eblk, psrc, ptgt, pblk, bound, dblk,
    gw1, ggain, gw2, ew1, egain, ew2, pw1, pgain, pw2, dw1, dgain, dw2, B, S,
):
    E = eblk.shape[2]
    PE = pblk.shape[2]
    rows = eblk.shape[-1]
    n, ch = grid_inputs.shape[2:]
    mrows, hw = emb.shape[2:]
    lat_w = 2 * hw
    g_blk = n // rows
    smem = pl.BlockSpec(memory_space=pltpu.SMEM)
    vmem = pl.BlockSpec(memory_space=pltpu.VMEM)
    hbm = pl.BlockSpec(memory_space=pl.ANY)
    dma = pltpu.SemaphoreType.DMA
    base, mall, dsum_w = pl.pallas_call(
        functools.partial(front_kernel, B, S, E, PE),
        out_shape=(
            jax.ShapeDtypeStruct((n, lat_w), BF16),
            jax.ShapeDtypeStruct((2, B, mrows, hw), BF16),
            jax.ShapeDtypeStruct((lat_w, lat_w), BF16),
        ),
        in_specs=[smem] * 6 + [vmem] * 6 + [hbm] * 8,
        out_specs=(vmem, vmem, vmem),
        scratch_shapes=[
            pltpu.VMEM((mrows, lat_w), BF16),
            pltpu.VMEM((ch, lat_w), BF16),
            pltpu.VMEM((lat_w, lat_w), BF16),
            pltpu.VMEM((2, lat_w, lat_w), BF16),
            pltpu.VMEM((lat_w, lat_w), BF16),
            pltpu.VMEM((2, lat_w, lat_w), BF16),
            pltpu.VMEM((lat_w, lat_w), BF16),
            pltpu.VMEM((lat_w, lat_w), BF16),
            pltpu.VMEM((2, g_blk, rows, hw), BF16),
            pltpu.VMEM((E * rows, hw), BF16),
            pltpu.VMEM((mrows, hw), F32),
            pltpu.VMEM((B - 1, mrows, hw), BF16),
            pltpu.VMEM((B - 1, mrows, hw), BF16),
            pltpu.VMEM((2, mrows, hw), BF16),
            pltpu.VMEM((2, mrows, hw), BF16),
            pltpu.VMEM((2, M_BLK, rows, hw), BF16),
            pltpu.VMEM((2, rows, hw), BF16),
            pltpu.VMEM((M_BLK + 2, rows, hw), BF16),
            pltpu.VMEM((mrows, lat_w), F32),
            dma((9,)), dma((9,)), dma((9,)),
            dma((B - 1,)), dma((B - 1,)),
            dma((2,)), dma((2,)), dma((2,)), dma((2,)),
            dma((B - 1,)), dma((B - 1,)), dma((B - 1,)), dma((B - 1,)),
        ],
        compiler_params=pltpu.CompilerParams(
            collective_id=0, has_side_effects=True, vmem_limit_bytes=48 * 2**20
        ),
    )(
        counts[0, 0], esrc[0, 0], etgt[0, 0], psrc[0, 0], ptgt[0, 0], bound.reshape(-1),
        grid_inputs[0, 0], eblk[0, 0], pblk[0, 0],
        ggain.reshape(1, -1), egain.reshape(1, -1), pgain.reshape(1, -1),
        emb[0, 0], gw1, gw2, ew1, ew2, pw1, pw2, dw1,
    )
    out = pl.pallas_call(
        functools.partial(back_kernel, B, E),
        out_shape=jax.ShapeDtypeStruct((n, ch), F32),
        in_specs=[smem] * 3 + [vmem] * 6,
        out_specs=vmem,
        scratch_shapes=[pltpu.VMEM((g_blk, rows, lat_w), F32)],
        compiler_params=pltpu.CompilerParams(vmem_limit_bytes=48 * 2**20),
    )(
        counts[0, 0], esrc[0, 0], etgt[0, 0],
        base, mall, dsum_w, dblk[0, 0], dgain.reshape(1, -1), dw2,
    )
    return out[None, None]


def solution(mesh):
    B, S = mesh.shape["band"], mesh.shape["sector"]
    idx = P("band", "sector", None)
    blk = P("band", "sector", None, None, None)
    rows = P(("groups", "band"), "sector", None, None)
    w3 = P(None, None, "chan")
    w2 = P(None, "chan")
    in_specs = (
        rows, P(("groups", "band"), "sector", None, "chan"),
        idx, idx, idx, blk, idx, idx, blk, P("band", "sector", None, None), blk,
        w2, P(), w2, w3, P(), w2, w3, P(), w2, w3, P(), P(),
    )
    return jax.shard_map(
        functools.partial(local, B=B, S=S),
        mesh=mesh, in_specs=in_specs, out_specs=rows, check_vma=False,
    )
```

```python
import functools

import jax
import jax.numpy as jnp
from jax import lax
from jax.experimental import pallas as pl
from jax.experimental.pallas import tpu as pltpu
from jax.sharding import PartitionSpec as P

MESH = pl.DeviceIdType.MESH
F32 = jnp.float32
BF16 = jnp.bfloat16
M_BLK = 2


def mm(a, b):
    return jnp.dot(a, b, preferred_element_type=F32)


def norm_silu(v, gain):
    n = 1.0 / v.shape[-1]
    center = v - jnp.sum(v, axis=-1, keepdims=True) * n
    spread = jnp.sum(center * center, axis=-1, keepdims=True) * n
    half = center * lax.rsqrt(spread + 1e-5) * (0.5 * gain)
    return (half + half * jnp.tanh(half)).astype(BF16)


def front_kernel(
    B, S, E, PE,
    counts, esrc, etgt, psrc, ptgt, bound,
    x, eblk, pblk, ggain, egain, pgain,
    emb, gw1, gw2, ew1, ew2, pw1, pw2, dw1,
    base, mall, dsum_w,
    emb_f, gw1_f, gw2_f, ew1_f, ew2_f, pw1_f, pw2_f, dw1_f,
    lat, xs, own, psend, precv, half_send, half_recv, m1, bsend, srcs, wide,
    loc_sem, wsend_sem, wrecv_sem, as_sem, ar_sem, hs_sem, hr_sem, bs_sem, br_sem,
    gs_sem, gr_sem, fs_sem, fr_sem,
):
    me = lax.axis_index("band")
    sec = lax.axis_index("sector")
    c = lax.axis_index("chan")
    oc = 1 - c
    hw = gw2.shape[-1]
    nxt = lax.rem(sec + 1, S)
    prv = lax.rem(sec + S - 1, S)
    mrows = emb.shape[0]
    rows = mrows // M_BLK
    g_blk = lat.shape[1]
    cols = pl.ds(pl.multiple_of(c * hw, hw), hw)
    ocols = pl.ds(pl.multiple_of(oc * hw, hw), hw)

    parts = [
        (gw1, gw1_f.at[:, cols]),
        (gw2, gw2_f.at[:, cols]),
        (emb, emb_f.at[:, cols]),
        (ew1, ew1_f.at[:, :, cols]),
        (dw1.at[0], dw1_f.at[:, cols]),
        (ew2, ew2_f.at[:, cols]),
        (pw1, pw1_f.at[:, :, cols]),
        (pw2, pw2_f.at[:, cols]),
        (dw1.at[1], dsum_w.at[:, cols]),
    ]
    local = [pltpu.make_async_copy(s, d, loc_sem.at[i]) for i, (s, d) in enumerate(parts)]
    for cp in local:
        cp.start()

    barrier = pltpu.get_barrier_semaphore()
    pl.semaphore_signal(barrier, inc=1, device_id={"chan": oc}, device_id_type=MESH)
    pl.semaphore_signal(barrier, inc=1, device_id={"sector": nxt}, device_id_type=MESH)
    pl.semaphore_signal(barrier, inc=1, device_id={"sector": prv}, device_id_type=MESH)
    for d in range(1, B):
        pl.semaphore_signal(
            barrier, inc=1, device_id={"band": lax.rem(me + d, B)}, device_id_type=MESH
        )
    pl.semaphore_wait(barrier, B + 2)

    remote = [
        pltpu.make_async_remote_copy(
            s, d, wsend_sem.at[i], wrecv_sem.at[i], device_id={"chan": oc}, device_id_type=MESH
        )
        for i, (s, d) in enumerate(parts)
    ]
    for cp in remote:
        cp.start()

    def arrived(i):
        local[i].wait()
        remote[i].wait_recv()

    arrived(0)
    arrived(1)

    chunk = 2 * rows

    def grid_step(i, _):
        r = pl.ds(pl.multiple_of(i * chunk, chunk), chunk)
        pre = lax.dot_general(
            x[:, r], gw1_f[...], (((0,), (0,)), ((), ())), preferred_element_type=F32
        )
        h = norm_silu(pre, ggain[...])
        latent = mm(h, gw2_f[...]).astype(BF16)
        for k in range(2):
            for j in range(2):
                lat[k, 2 * i + j] = latent[j * rows : (j + 1) * rows, k * hw : (k + 1) * hw]
        return 0

    lax.fori_loop(0, g_blk // 2, grid_step, 0, unroll=2)

    for e in range(E):
        xs[e * rows : (e + 1) * rows, :] = lat[c, esrc[e]]

    def part_for(q):
        lo = jnp.int32(0)
        size = jnp.int32(0)
        for p in range(B):
            lo = lo + jnp.where(p < q, counts[p], 0)
            size = size + jnp.where(p == q, counts[p], 0)
        acc = []
        for m in range(M_BLK):
            pieces = []
            for e in range(E):
                keep = jnp.where((lo <= e) & (e < lo + size) & (etgt[e] == m), 1.0, 0.0)
                pieces.append(eblk[e] * keep.astype(BF16))
            acc.append(mm(jnp.concatenate(pieces, axis=1), xs[...]))
        return acc

    def band_copy(d):
        return pltpu.make_async_remote_copy(
            psend.at[d - 1], precv.at[d - 1], as_sem.at[d - 1], ar_sem.at[d - 1],
            device_id={"band": lax.rem(me + d, B)}, device_id_type=MESH,
        )

    def send_step(d, _):
        acc = part_for(lax.rem(me + d, B))
        for m in range(M_BLK):
            psend[d - 1, m * rows : (m + 1) * rows, :] = acc[m].astype(BF16)
        band_copy(d).start()
        return 0

    lax.fori_loop(1, B, send_step, 0, unroll=B <= 4)
    acc = part_for(me)
    for m in range(M_BLK):
        own[m * rows : (m + 1) * rows, :] = acc[m]

    arrived(2)
    arrived(3)
    wide[...] = mm(emb_f[...], ew1_f[0])
    arrived(4)

    def base_step(i, _):
        left = jnp.concatenate([lat[0, 2 * i], lat[0, 2 * i + 1]], axis=0)
        right = jnp.concatenate([lat[1, 2 * i], lat[1, 2 * i + 1]], axis=0)
        out = mm(left, dw1_f[:hw, :]) + mm(right, dw1_f[hw:, :])
        base[pl.ds(pl.multiple_of(i * chunk, chunk), chunk), :] = out.astype(BF16)
        return 0

    lax.fori_loop(0, g_blk // 2, base_step, 0)

    def take_step(d, _):
        band_copy(d).wait_recv()
        own[...] += precv[d - 1].astype(F32)
        return 0

    lax.fori_loop(1, B, take_step, 0, unroll=B <= 4)

    def update(k, summed, w1, gain, w2):
        half_send[k] = summed.astype(BF16)
        cp = pltpu.make_async_remote_copy(
            half_send.at[k], half_recv.at[k], hs_sem.at[k], hr_sem.at[k],
            device_id={"chan": oc}, device_id_type=MESH,
        )
        cp.start()
        pre = wide[...] + mm(half_send[k], w1[1, cols, :])
        cp.wait_recv()
        pre = pre + mm(half_recv[k], w1[1, ocols, :])
        cp.wait_send()
        return mm(norm_silu(pre, gain[...]), w2[...])

    arrived(5)
    one = (emb_f[...].astype(F32) + update(0, own[...], ew1_f, egain, ew2_f)).astype(BF16)
    for k in range(2):
        for j in range(M_BLK):
            m1[k, j] = one[j * rows : (j + 1) * rows, k * hw : (k + 1) * hw]
    bsend[0] = m1[c, bound[0]]
    bsend[1] = m1[c, bound[1]]
    to_next = pltpu.make_async_remote_copy(
        bsend.at[1], srcs.at[M_BLK], bs_sem.at[1], br_sem.at[0],
        device_id={"sector": nxt}, device_id_type=MESH,
    )
    to_prev = pltpu.make_async_remote_copy(
        bsend.at[0], srcs.at[M_BLK + 1], bs_sem.at[0], br_sem.at[1],
        device_id={"sector": prv}, device_id_type=MESH,
    )
    to_next.start()
    to_prev.start()
    for j in range(M_BLK):
        srcs[j] = m1[c, j]
    arrived(6)
    wide[...] = mm(one, pw1_f[0])
    to_next.wait_recv()
    to_prev.wait_recv()
    ys = jnp.concatenate([srcs[psrc[e]] for e in range(PE)], axis=0)
    for m in range(M_BLK):
        pieces = []
        for e in range(PE):
            keep = jnp.where(ptgt[e] == m, 1.0, 0.0)
            pieces.append(pblk[e] * keep.astype(BF16))
        own[m * rows : (m + 1) * rows, :] = mm(jnp.concatenate(pieces, axis=1), ys)
    arrived(7)
    two = (one.astype(F32) + update(1, own[...], pw1_f, pgain, pw2_f)).astype(BF16)
    for k in range(2):
        mall[k, me] = two[:, k * hw : (k + 1) * hw]

    def out_copy(d):
        return pltpu.make_async_remote_copy(
            mall.at[c, me], mall.at[c, me], gs_sem.at[d - 1], gr_sem.at[d - 1],
            device_id={"band": lax.rem(me + d, B)}, device_id_type=MESH,
        )

    def in_copy(d):
        src = lax.rem(me - d + B, B)
        return pltpu.make_async_remote_copy(
            mall.at[c, src], mall.at[c, src], gs_sem.at[d - 1], gr_sem.at[d - 1],
            device_id={"band": lax.rem(me + d, B)}, device_id_type=MESH,
        )

    def forward(d, half):
        src = lax.rem(me - d + B, B)
        return pltpu.make_async_remote_copy(
            mall.at[half, src], mall.at[half, src], fs_sem.at[d - 1], fr_sem.at[d - 1],
            device_id={"chan": oc}, device_id_type=MESH,
        )

    def gather_start(d, _):
        out_copy(d).start()
        return 0

    def gather_pass(d, _):
        in_copy(d).wait_recv()
        forward(d, c).start()
        return 0

    def gather_end(d, _):
        forward(d, oc).wait_recv()
        forward(d, c).wait_send()
        out_copy(d).wait_send()
        band_copy(d).wait_send()
        return 0

    lax.fori_loop(1, B, gather_start, 0, unroll=B <= 4)
    arrived(8)
    to_next.wait_send()
    to_prev.wait_send()
    for cp in remote:
        cp.wait_send()
    lax.fori_loop(1, B, gather_pass, 0, unroll=B <= 4)
    lax.fori_loop(1, B, gather_end, 0, unroll=B <= 4)


def back_kernel(B, E, counts, esrc, etgt, base, mall, dsum_w, dblk, dgain, dw2, out, acc):
    rows = dblk.shape[1]
    g_blk = acc.shape[0]
    hw = mall.shape[-1]
    for g in range(g_blk):
        acc[g] = base[g * rows : (g + 1) * rows, :].astype(F32)

    def edge(e, _):
        peer = jnp.int32(0)
        end = jnp.int32(0)
        for p in range(B):
            end = end + counts[p]
            peer = peer + jnp.where(end <= e, 1, 0)
        r = pl.ds(pl.multiple_of(etgt[e] * rows, rows), rows)
        add = jnp.zeros((rows, 2 * hw), F32)
        for k in range(2):
            msg = mm(dblk[e], mall[k, peer, r, :]).astype(BF16)
            add = add + mm(msg, dsum_w[k * hw : (k + 1) * hw, :])
        acc[esrc[e]] += add
        return 0

    lax.fori_loop(0, E, edge, 0, unroll=4)

    def final(i, _):
        v = jnp.concatenate([acc[2 * i], acc[2 * i + 1]], axis=0)
        h = norm_silu(v, dgain[...])
        r = pl.ds(pl.multiple_of(i * 2 * rows, 2 * rows), 2 * rows)
        out[:, 0, r] = lax.dot_general(
            dw2[...], h, (((1,), (1,)), ((), ())), preferred_element_type=F32
        )
        return 0

    lax.fori_loop(0, g_blk // 2, final, 0, unroll=2)


def local(
    grid_inputs, emb, counts, esrc, etgt, eblk, psrc, ptgt, pblk, bound, dblk,
    gw1, ggain, gw2, ew1, egain, ew2, pw1, pgain, pw2, dw1, dgain, dw2, B, S,
):
    E = eblk.shape[2]
    PE = pblk.shape[2]
    rows = eblk.shape[-1]
    n, ch = grid_inputs.shape[2:]
    mrows, hw = emb.shape[2:]
    lat_w = 2 * hw
    g_blk = n // rows
    smem = pl.BlockSpec(memory_space=pltpu.SMEM)
    vmem = pl.BlockSpec(memory_space=pltpu.VMEM)
    hbm = pl.BlockSpec(memory_space=pl.ANY)
    dma = pltpu.SemaphoreType.DMA
    base, mall, dsum_w = pl.pallas_call(
        functools.partial(front_kernel, B, S, E, PE),
        out_shape=(
            jax.ShapeDtypeStruct((n, lat_w), BF16),
            jax.ShapeDtypeStruct((2, B, mrows, hw), BF16),
            jax.ShapeDtypeStruct((lat_w, lat_w), BF16),
        ),
        in_specs=[smem] * 6 + [vmem] * 6 + [hbm] * 8,
        out_specs=(vmem, vmem, vmem),
        scratch_shapes=[
            pltpu.VMEM((mrows, lat_w), BF16),
            pltpu.VMEM((ch, lat_w), BF16),
            pltpu.VMEM((lat_w, lat_w), BF16),
            pltpu.VMEM((2, lat_w, lat_w), BF16),
            pltpu.VMEM((lat_w, lat_w), BF16),
            pltpu.VMEM((2, lat_w, lat_w), BF16),
            pltpu.VMEM((lat_w, lat_w), BF16),
            pltpu.VMEM((lat_w, lat_w), BF16),
            pltpu.VMEM((2, g_blk, rows, hw), BF16),
            pltpu.VMEM((E * rows, hw), BF16),
            pltpu.VMEM((mrows, hw), F32),
            pltpu.VMEM((B - 1, mrows, hw), BF16),
            pltpu.VMEM((B - 1, mrows, hw), BF16),
            pltpu.VMEM((2, mrows, hw), BF16),
            pltpu.VMEM((2, mrows, hw), BF16),
            pltpu.VMEM((2, M_BLK, rows, hw), BF16),
            pltpu.VMEM((2, rows, hw), BF16),
            pltpu.VMEM((M_BLK + 2, rows, hw), BF16),
            pltpu.VMEM((mrows, lat_w), F32),
            dma((9,)), dma((9,)), dma((9,)),
            dma((B - 1,)), dma((B - 1,)),
            dma((2,)), dma((2,)), dma((2,)), dma((2,)),
            dma((B - 1,)), dma((B - 1,)), dma((B - 1,)), dma((B - 1,)),
        ],
        compiler_params=pltpu.CompilerParams(
            collective_id=0, has_side_effects=True, vmem_limit_bytes=63 * 2**20
        ),
    )(
        counts[0, 0], esrc[0, 0], etgt[0, 0], psrc[0, 0], ptgt[0, 0], bound.reshape(-1),
        grid_inputs[0, 0].T, eblk[0, 0], pblk[0, 0],
        ggain.reshape(1, -1), egain.reshape(1, -1), pgain.reshape(1, -1),
        emb[0, 0], gw1, gw2, ew1, ew2, pw1, pw2, dw1,
    )
    out = pl.pallas_call(
        functools.partial(back_kernel, B, E),
        out_shape=jax.ShapeDtypeStruct((ch, 1, n), F32),
        in_specs=[smem] * 3 + [vmem] * 6,
        out_specs=vmem,
        scratch_shapes=[pltpu.VMEM((g_blk, rows, lat_w), F32)],
        compiler_params=pltpu.CompilerParams(vmem_limit_bytes=63 * 2**20),
    )(
        counts[0, 0], esrc[0, 0], etgt[0, 0],
        base, mall, dsum_w, dblk[0, 0], dgain.reshape(1, -1), dw2.T,
    )
    return jnp.transpose(out, (1, 2, 0))[None]


def solution(mesh):
    B, S = mesh.shape["band"], mesh.shape["sector"]
    idx = P("band", "sector", None)
    blk = P("band", "sector", None, None, None)
    rows = P(("groups", "band"), "sector", None, None)
    w3 = P(None, None, "chan")
    w2 = P(None, "chan")
    in_specs = (
        rows, P(("groups", "band"), "sector", None, "chan"),
        idx, idx, idx, blk, idx, idx, blk, P("band", "sector", None, None), blk,
        w2, P(), w2, w3, P(), w2, w3, P(), w2, w3, P(), P(),
    )
    return jax.shard_map(
        functools.partial(local, B=B, S=S),
        mesh=mesh, in_specs=in_specs, out_specs=rows, check_vma=False,
    )
```

```python
import functools

import jax
import jax.numpy as jnp
from jax import lax
from jax.experimental import pallas as pl
from jax.experimental.pallas import tpu as pltpu
from jax.sharding import PartitionSpec as P

MESH = pl.DeviceIdType.MESH
F32 = jnp.float32
BF16 = jnp.bfloat16
M_BLK = 2


def mm(a, b):
    return jnp.dot(a, b, preferred_element_type=F32)


def norm_silu(v, gain):
    n = 1.0 / v.shape[-1]
    center = v - jnp.sum(v, axis=-1, keepdims=True) * n
    spread = jnp.sum(center * center, axis=-1, keepdims=True) * n
    half = center * lax.rsqrt(spread + 1e-5) * (0.5 * gain)
    return (half + half * jnp.tanh(half)).astype(BF16)


def front_kernel(
    B, S, E, PE,
    counts, esrc, etgt, psrc, ptgt, bound,
    x, eblk, pblk, ggain, egain, pgain,
    emb, gw1, gw2, ew1, ew2, pw1, pw2, dw1,
    base, mall, dsum_w,
    emb_f, gw1_f, gw2_f, ew1_f, ew2_f, pw1_f, pw2_f, dw1_f,
    xb, xs, own, psend, precv, half_send, half_recv, m1, bsend, srcs, wide,
    loc_sem, wsend_sem, wrecv_sem, as_sem, ar_sem, hs_sem, hr_sem, bs_sem, br_sem,
    gs_sem, gr_sem, fs_sem, fr_sem,
):
    me = lax.axis_index("band")
    sec = lax.axis_index("sector")
    c = lax.axis_index("chan")
    oc = 1 - c
    hw = gw2.shape[-1]
    nxt = lax.rem(sec + 1, S)
    prv = lax.rem(sec + S - 1, S)
    mrows = emb.shape[0]
    rows = mrows // M_BLK
    cols = pl.ds(pl.multiple_of(c * hw, hw), hw)
    ocols = pl.ds(pl.multiple_of(oc * hw, hw), hw)

    parts = [
        (gw1, gw1_f.at[:, cols]),
        (gw2, gw2_f.at[:, cols]),
        (emb, emb_f.at[:, cols]),
        (ew1, ew1_f.at[:, :, cols]),
        (dw1.at[0], dw1_f.at[:, cols]),
        (ew2, ew2_f.at[:, cols]),
        (pw1, pw1_f.at[:, :, cols]),
        (pw2, pw2_f.at[:, cols]),
        (dw1.at[1], dsum_w.at[:, cols]),
    ]
    local = [pltpu.make_async_copy(s, d, loc_sem.at[i]) for i, (s, d) in enumerate(parts)]
    for cp in local:
        cp.start()

    barrier = pltpu.get_barrier_semaphore()
    pl.semaphore_signal(barrier, inc=1, device_id={"chan": oc}, device_id_type=MESH)
    pl.semaphore_signal(barrier, inc=1, device_id={"sector": nxt}, device_id_type=MESH)
    pl.semaphore_signal(barrier, inc=1, device_id={"sector": prv}, device_id_type=MESH)
    for d in range(1, B):
        pl.semaphore_signal(
            barrier, inc=1, device_id={"band": lax.rem(me + d, B)}, device_id_type=MESH
        )
    for g in range(x.shape[1] // rows):
        xb[g] = x[:, g * rows : (g + 1) * rows]
    pl.semaphore_wait(barrier, B + 2)

    remote = [
        pltpu.make_async_remote_copy(
            s, d, wsend_sem.at[i], wrecv_sem.at[i], device_id={"chan": oc}, device_id_type=MESH
        )
        for i, (s, d) in enumerate(parts)
    ]
    for cp in remote:
        cp.start()

    def arrived(i):
        local[i].wait()
        remote[i].wait_recv()

    def hidden(left):
        pre = lax.dot_general(
            left, gw1_f[...], (((0,), (0,)), ((), ())), preferred_element_type=F32
        )
        return norm_silu(pre, ggain[...])

    chunk = 2 * rows
    local[1].wait()
    arrived(0)

    for e in range(0, E, 2):
        left = jnp.concatenate([xb[esrc[e]], xb[esrc[e + 1]]], axis=1)
        xs[e * rows : (e + 2) * rows, :] = mm(hidden(left), gw2_f[:, cols]).astype(BF16)

    def part_for(q):
        lo = jnp.int32(0)
        size = jnp.int32(0)
        for p in range(B):
            lo = lo + jnp.where(p < q, counts[p], 0)
            size = size + jnp.where(p == q, counts[p], 0)
        acc = []
        for m in range(M_BLK):
            pieces = []
            for e in range(E):
                keep = jnp.where((lo <= e) & (e < lo + size) & (etgt[e] == m), 1.0, 0.0)
                pieces.append(eblk[e] * keep.astype(BF16))
            acc.append(mm(jnp.concatenate(pieces, axis=1), xs[...]))
        return acc

    def band_copy(d):
        return pltpu.make_async_remote_copy(
            psend.at[d - 1], precv.at[d - 1], as_sem.at[d - 1], ar_sem.at[d - 1],
            device_id={"band": lax.rem(me + d, B)}, device_id_type=MESH,
        )

    def send_step(d, _):
        acc = part_for(lax.rem(me + d, B))
        for m in range(M_BLK):
            psend[d - 1, m * rows : (m + 1) * rows, :] = acc[m].astype(BF16)
        band_copy(d).start()
        return 0

    lax.fori_loop(1, B, send_step, 0, unroll=B <= 4)
    acc = part_for(me)
    for m in range(M_BLK):
        own[m * rows : (m + 1) * rows, :] = acc[m]

    arrived(2)
    arrived(3)
    wide[...] = mm(emb_f[...], ew1_f[0])
    remote[1].wait_recv()
    arrived(4)

    def base_step(i, _):
        r = pl.ds(pl.multiple_of(i * chunk, chunk), chunk)
        latent = mm(hidden(x[:, r]), gw2_f[...]).astype(BF16)
        base[r, :] = mm(latent, dw1_f[...]).astype(BF16)
        return 0

    lax.fori_loop(0, x.shape[1] // chunk, base_step, 0, unroll=2)

    def take_step(d, _):
        band_copy(d).wait_recv()
        own[...] += precv[d - 1].astype(F32)
        return 0

    lax.fori_loop(1, B, take_step, 0, unroll=B <= 4)

    def update(k, summed, w1, gain, w2):
        half_send[k] = summed.astype(BF16)
        cp = pltpu.make_async_remote_copy(
            half_send.at[k], half_recv.at[k], hs_sem.at[k], hr_sem.at[k],
            device_id={"chan": oc}, device_id_type=MESH,
        )
        cp.start()
        pre = wide[...] + mm(half_send[k], w1[1, cols, :])
        cp.wait_recv()
        pre = pre + mm(half_recv[k], w1[1, ocols, :])
        cp.wait_send()
        return mm(norm_silu(pre, gain[...]), w2[...])

    arrived(5)
    one = (emb_f[...].astype(F32) + update(0, own[...], ew1_f, egain, ew2_f)).astype(BF16)
    for k in range(2):
        for j in range(M_BLK):
            m1[k, j] = one[j * rows : (j + 1) * rows, k * hw : (k + 1) * hw]
    bsend[0] = m1[c, bound[0]]
    bsend[1] = m1[c, bound[1]]
    to_next = pltpu.make_async_remote_copy(
        bsend.at[1], srcs.at[M_BLK], bs_sem.at[1], br_sem.at[0],
        device_id={"sector": nxt}, device_id_type=MESH,
    )
    to_prev = pltpu.make_async_remote_copy(
        bsend.at[0], srcs.at[M_BLK + 1], bs_sem.at[0], br_sem.at[1],
        device_id={"sector": prv}, device_id_type=MESH,
    )
    to_next.start()
    to_prev.start()
    for j in range(M_BLK):
        srcs[j] = m1[c, j]
    arrived(6)
    wide[...] = mm(one, pw1_f[0])
    to_next.wait_recv()
    to_prev.wait_recv()
    ys = jnp.concatenate([srcs[psrc[e]] for e in range(PE)], axis=0)
    for m in range(M_BLK):
        pieces = []
        for e in range(PE):
            keep = jnp.where(ptgt[e] == m, 1.0, 0.0)
            pieces.append(pblk[e] * keep.astype(BF16))
        own[m * rows : (m + 1) * rows, :] = mm(jnp.concatenate(pieces, axis=1), ys)
    arrived(7)
    two = (one.astype(F32) + update(1, own[...], pw1_f, pgain, pw2_f)).astype(BF16)
    for k in range(2):
        mall[k, me] = two[:, k * hw : (k + 1) * hw]

    def out_copy(d):
        return pltpu.make_async_remote_copy(
            mall.at[c, me], mall.at[c, me], gs_sem.at[d - 1], gr_sem.at[d - 1],
            device_id={"band": lax.rem(me + d, B)}, device_id_type=MESH,
        )

    def in_copy(d):
        src = lax.rem(me - d + B, B)
        return pltpu.make_async_remote_copy(
            mall.at[c, src], mall.at[c, src], gs_sem.at[d - 1], gr_sem.at[d - 1],
            device_id={"band": lax.rem(me + d, B)}, device_id_type=MESH,
        )

    def forward(d, half):
        src = lax.rem(me - d + B, B)
        return pltpu.make_async_remote_copy(
            mall.at[half, src], mall.at[half, src], fs_sem.at[d - 1], fr_sem.at[d - 1],
            device_id={"chan": oc}, device_id_type=MESH,
        )

    def gather_start(d, _):
        out_copy(d).start()
        return 0

    def gather_pass(d, _):
        in_copy(d).wait_recv()
        forward(d, c).start()
        return 0

    def gather_end(d, _):
        forward(d, oc).wait_recv()
        forward(d, c).wait_send()
        out_copy(d).wait_send()
        band_copy(d).wait_send()
        return 0

    lax.fori_loop(1, B, gather_start, 0, unroll=B <= 4)
    arrived(8)
    to_next.wait_send()
    to_prev.wait_send()
    for cp in remote:
        cp.wait_send()
    lax.fori_loop(1, B, gather_pass, 0, unroll=B <= 4)
    lax.fori_loop(1, B, gather_end, 0, unroll=B <= 4)


def back_kernel(B, E, counts, esrc, etgt, base, mall, dsum_w, dblk, dgain, dw2, out, acc):
    rows = dblk.shape[1]
    hw = mall.shape[-1]
    step = pl.program_id(0)
    held = base.shape[0] // rows

    @pl.when(step == 0)
    def _():
        acc[...] = jnp.zeros_like(acc)

        def edge(e, _):
            peer = jnp.int32(0)
            end = jnp.int32(0)
            for p in range(B):
                end = end + counts[p]
                peer = peer + jnp.where(end <= e, 1, 0)
            r = pl.ds(pl.multiple_of(etgt[e] * rows, rows), rows)
            add = jnp.zeros((rows, 2 * hw), F32)
            for k in range(2):
                msg = mm(dblk[e], mall[k, peer, r, :]).astype(BF16)
                add = add + mm(msg, dsum_w[k * hw : (k + 1) * hw, :])
            acc[esrc[e]] += add
            return 0

        lax.fori_loop(0, E, edge, 0, unroll=4)

    for i in range(held // 2):
        r = pl.ds(i * 2 * rows, 2 * rows)
        g = step * held + 2 * i
        v = base[r, :].astype(F32) + jnp.concatenate([acc[g], acc[g + 1]], axis=0)
        out[:, 0, r] = lax.dot_general(
            dw2[...], norm_silu(v, dgain[...]), (((1,), (1,)), ((), ())),
            preferred_element_type=F32,
        )


def local(
    grid_inputs, emb, counts, esrc, etgt, eblk, psrc, ptgt, pblk, bound, dblk,
    gw1, ggain, gw2, ew1, egain, ew2, pw1, pgain, pw2, dw1, dgain, dw2, B, S,
):
    E = eblk.shape[2]
    PE = pblk.shape[2]
    rows = eblk.shape[-1]
    n, ch = grid_inputs.shape[2:]
    mrows, hw = emb.shape[2:]
    lat_w = 2 * hw
    g_blk = n // rows
    smem = pl.BlockSpec(memory_space=pltpu.SMEM)
    vmem = pl.BlockSpec(memory_space=pltpu.VMEM)
    hbm = pl.BlockSpec(memory_space=pl.ANY)
    dma = pltpu.SemaphoreType.DMA
    base, mall, dsum_w = pl.pallas_call(
        functools.partial(front_kernel, B, S, E, PE),
        out_shape=(
            jax.ShapeDtypeStruct((n, lat_w), BF16),
            jax.ShapeDtypeStruct((2, B, mrows, hw), BF16),
            jax.ShapeDtypeStruct((lat_w, lat_w), BF16),
        ),
        in_specs=[smem] * 6 + [vmem] * 6 + [hbm] * 8,
        out_specs=(vmem, vmem, vmem),
        scratch_shapes=[
            pltpu.VMEM((mrows, lat_w), BF16),
            pltpu.VMEM((ch, lat_w), BF16),
            pltpu.VMEM((lat_w, lat_w), BF16),
            pltpu.VMEM((2, lat_w, lat_w), BF16),
            pltpu.VMEM((lat_w, lat_w), BF16),
            pltpu.VMEM((2, lat_w, lat_w), BF16),
            pltpu.VMEM((lat_w, lat_w), BF16),
            pltpu.VMEM((lat_w, lat_w), BF16),
            pltpu.VMEM((g_blk, ch, rows), BF16),
            pltpu.VMEM((E * rows, hw), BF16),
            pltpu.VMEM((mrows, hw), F32),
            pltpu.VMEM((B - 1, mrows, hw), BF16),
            pltpu.VMEM((B - 1, mrows, hw), BF16),
            pltpu.VMEM((2, mrows, hw), BF16),
            pltpu.VMEM((2, mrows, hw), BF16),
            pltpu.VMEM((2, M_BLK, rows, hw), BF16),
            pltpu.VMEM((2, rows, hw), BF16),
            pltpu.VMEM((M_BLK + 2, rows, hw), BF16),
            pltpu.VMEM((mrows, lat_w), F32),
            dma((9,)), dma((9,)), dma((9,)),
            dma((B - 1,)), dma((B - 1,)),
            dma((2,)), dma((2,)), dma((2,)), dma((2,)),
            dma((B - 1,)), dma((B - 1,)), dma((B - 1,)), dma((B - 1,)),
        ],
        compiler_params=pltpu.CompilerParams(
            collective_id=0, has_side_effects=True, vmem_limit_bytes=63 * 2**20
        ),
    )(
        counts[0, 0], esrc[0, 0], etgt[0, 0], psrc[0, 0], ptgt[0, 0], bound.reshape(-1),
        grid_inputs[0, 0].T, eblk[0, 0], pblk[0, 0],
        ggain.reshape(1, -1), egain.reshape(1, -1), pgain.reshape(1, -1),
        emb[0, 0], gw1, gw2, ew1, ew2, pw1, pw2, dw1,
    )
    out = pl.pallas_call(
        functools.partial(back_kernel, B, E),
        out_shape=jax.ShapeDtypeStruct((ch, 1, n), F32),
        grid=(4,),
        in_specs=[smem] * 3 + [pl.BlockSpec((n // 4, lat_w), lambda i: (i, 0))] + [vmem] * 5,
        out_specs=pl.BlockSpec((ch, 1, n // 4), lambda i: (0, 0, i)),
        scratch_shapes=[pltpu.VMEM((g_blk, rows, lat_w), F32)],
        compiler_params=pltpu.CompilerParams(vmem_limit_bytes=63 * 2**20),
    )(
        counts[0, 0], esrc[0, 0], etgt[0, 0],
        base, mall, dsum_w, dblk[0, 0], dgain.reshape(1, -1), dw2.T,
    )
    return jnp.transpose(out, (1, 2, 0))[None]


def solution(mesh):
    B, S = mesh.shape["band"], mesh.shape["sector"]
    idx = P("band", "sector", None)
    blk = P("band", "sector", None, None, None)
    rows = P(("groups", "band"), "sector", None, None)
    w3 = P(None, None, "chan")
    w2 = P(None, "chan")
    in_specs = (
        rows, P(("groups", "band"), "sector", None, "chan"),
        idx, idx, idx, blk, idx, idx, blk, P("band", "sector", None, None), blk,
        w2, P(), w2, w3, P(), w2, w3, P(), w2, w3, P(), P(),
    )
    return jax.shard_map(
        functools.partial(local, B=B, S=S),
        mesh=mesh, in_specs=in_specs, out_specs=rows, check_vma=False,
    )
```

```python
import functools

import jax
import jax.numpy as jnp
from jax import lax
from jax.experimental import pallas as pl
from jax.experimental.pallas import tpu as pltpu
from jax.sharding import PartitionSpec as P

MESH = pl.DeviceIdType.MESH
F32 = jnp.float32
BF16 = jnp.bfloat16
M_BLK = 2


def mm(a, b):
    return jnp.dot(a, b, preferred_element_type=F32)


def norm_silu(v, gain):
    n = 1.0 / v.shape[-1]
    center = v - jnp.sum(v, axis=-1, keepdims=True) * n
    spread = jnp.sum(center * center, axis=-1, keepdims=True) * n
    half = center * lax.rsqrt(spread + 1e-5) * (0.5 * gain)
    return (half + half * jnp.tanh(half)).astype(BF16)


def front_kernel(
    B, S, E, PE,
    counts, esrc, etgt, psrc, ptgt, bound,
    ggain, egain, pgain,
    x_in, eblk_in, pblk_in, emb, gw1, gw2, ew1, ew2, pw1, pw2, dw1,
    base_out, mall,
    x, eblk, pblk, base, dsum_w,
    emb_f, gw1_f, gw2_f, ew1_f, ew2_f, pw1_f, pw2_f, dw1_f,
    xb, xs, own, psend, precv, half_send, half_recv, m1, bsend, srcs, wide,
    in_sem, loc_sem, wsend_sem, wrecv_sem, as_sem, ar_sem, hs_sem, hr_sem, bs_sem, br_sem,
    gs_sem, gr_sem, fs_sem, fr_sem,
):
    me = lax.axis_index("band")
    sec = lax.axis_index("sector")
    c = lax.axis_index("chan")
    oc = 1 - c
    hw = gw2.shape[-1]
    nxt = lax.rem(sec + 1, S)
    prv = lax.rem(sec + S - 1, S)
    mrows = emb.shape[0]
    rows = mrows // M_BLK
    cols = pl.ds(pl.multiple_of(c * hw, hw), hw)
    ocols = pl.ds(pl.multiple_of(oc * hw, hw), hw)

    parts = [
        (gw1, gw1_f.at[:, cols]),
        (gw2, gw2_f.at[:, cols]),
        (emb, emb_f.at[:, cols]),
        (ew1, ew1_f.at[:, :, cols]),
        (dw1.at[0], dw1_f.at[:, cols]),
        (ew2, ew2_f.at[:, cols]),
        (pw1, pw1_f.at[:, :, cols]),
        (pw2, pw2_f.at[:, cols]),
        (dw1.at[1], dsum_w.at[:, cols]),
    ]
    local = [pltpu.make_async_copy(s, d, loc_sem.at[i]) for i, (s, d) in enumerate(parts)]
    operands = [
        pltpu.make_async_copy(s, d, in_sem.at[i])
        for i, (s, d) in enumerate([(x_in, x), (eblk_in, eblk), (pblk_in, pblk)])
    ]
    for cp in operands[:1] + local + operands[1:]:
        cp.start()

    barrier = pltpu.get_barrier_semaphore()
    pl.semaphore_signal(barrier, inc=1, device_id={"chan": oc}, device_id_type=MESH)
    pl.semaphore_signal(barrier, inc=1, device_id={"sector": nxt}, device_id_type=MESH)
    pl.semaphore_signal(barrier, inc=1, device_id={"sector": prv}, device_id_type=MESH)
    for d in range(1, B):
        pl.semaphore_signal(
            barrier, inc=1, device_id={"band": lax.rem(me + d, B)}, device_id_type=MESH
        )
    operands[0].wait()
    for g in range(x.shape[1] // rows):
        xb[g] = x[:, g * rows : (g + 1) * rows]
    pl.semaphore_wait(barrier, B + 2)

    remote = [
        pltpu.make_async_remote_copy(
            s, d, wsend_sem.at[i], wrecv_sem.at[i], device_id={"chan": oc}, device_id_type=MESH
        )
        for i, (s, d) in enumerate(parts)
    ]
    for cp in remote:
        cp.start()

    def arrived(i):
        local[i].wait()
        remote[i].wait_recv()

    def hidden(left):
        pre = lax.dot_general(
            left, gw1_f[...], (((0,), (0,)), ((), ())), preferred_element_type=F32
        )
        return norm_silu(pre, ggain[...])

    chunk = 2 * rows
    local[1].wait()
    arrived(0)

    for e in range(0, E, 2):
        left = jnp.concatenate([xb[esrc[e]], xb[esrc[e + 1]]], axis=1)
        xs[e * rows : (e + 2) * rows, :] = mm(hidden(left), gw2_f[:, cols]).astype(BF16)

    operands[1].wait()

    def part_for(q):
        lo = jnp.int32(0)
        size = jnp.int32(0)
        for p in range(B):
            lo = lo + jnp.where(p < q, counts[p], 0)
            size = size + jnp.where(p == q, counts[p], 0)
        acc = []
        for m in range(M_BLK):
            pieces = []
            for e in range(E):
                keep = jnp.where((lo <= e) & (e < lo + size) & (etgt[e] == m), 1.0, 0.0)
                pieces.append(eblk[e] * keep.astype(BF16))
            acc.append(mm(jnp.concatenate(pieces, axis=1), xs[...]))
        return acc

    def band_copy(d):
        return pltpu.make_async_remote_copy(
            psend.at[d - 1], precv.at[d - 1], as_sem.at[d - 1], ar_sem.at[d - 1],
            device_id={"band": lax.rem(me + d, B)}, device_id_type=MESH,
        )

    def send_step(d, _):
        acc = part_for(lax.rem(me + d, B))
        for m in range(M_BLK):
            psend[d - 1, m * rows : (m + 1) * rows, :] = acc[m].astype(BF16)
        band_copy(d).start()
        return 0

    lax.fori_loop(1, B, send_step, 0, unroll=B <= 4)
    acc = part_for(me)
    for m in range(M_BLK):
        own[m * rows : (m + 1) * rows, :] = acc[m]

    arrived(2)
    arrived(3)
    wide[...] = mm(emb_f[...], ew1_f[0])
    remote[1].wait_recv()
    arrived(4)

    def base_step(i, _):
        r = pl.ds(pl.multiple_of(i * chunk, chunk), chunk)
        latent = mm(hidden(x[:, r]), gw2_f[...]).astype(BF16)
        base[r, :] = mm(latent, dw1_f[...]).astype(BF16)
        return 0

    lax.fori_loop(0, x.shape[1] // chunk, base_step, 0, unroll=2)

    save = pltpu.make_async_copy(base, base_out, in_sem.at[3])
    save.start()

    def take_step(d, _):
        band_copy(d).wait_recv()
        own[...] += precv[d - 1].astype(F32)
        return 0

    lax.fori_loop(1, B, take_step, 0, unroll=B <= 4)

    def update(k, summed, w1, gain, w2):
        half_send[k] = summed.astype(BF16)
        cp = pltpu.make_async_remote_copy(
            half_send.at[k], half_recv.at[k], hs_sem.at[k], hr_sem.at[k],
            device_id={"chan": oc}, device_id_type=MESH,
        )
        cp.start()
        pre = wide[...] + mm(half_send[k], w1[1, cols, :])
        cp.wait_recv()
        pre = pre + mm(half_recv[k], w1[1, ocols, :])
        cp.wait_send()
        return mm(norm_silu(pre, gain[...]), w2[...])

    arrived(5)
    one = (emb_f[...].astype(F32) + update(0, own[...], ew1_f, egain, ew2_f)).astype(BF16)
    for k in range(2):
        for j in range(M_BLK):
            m1[k, j] = one[j * rows : (j + 1) * rows, k * hw : (k + 1) * hw]
    bsend[0] = m1[c, bound[0]]
    bsend[1] = m1[c, bound[1]]
    to_next = pltpu.make_async_remote_copy(
        bsend.at[1], srcs.at[M_BLK], bs_sem.at[1], br_sem.at[0],
        device_id={"sector": nxt}, device_id_type=MESH,
    )
    to_prev = pltpu.make_async_remote_copy(
        bsend.at[0], srcs.at[M_BLK + 1], bs_sem.at[0], br_sem.at[1],
        device_id={"sector": prv}, device_id_type=MESH,
    )
    to_next.start()
    to_prev.start()
    for j in range(M_BLK):
        srcs[j] = m1[c, j]
    arrived(6)
    wide[...] = mm(one, pw1_f[0])
    to_next.wait_recv()
    to_prev.wait_recv()
    operands[2].wait()
    ys = jnp.concatenate([srcs[psrc[e]] for e in range(PE)], axis=0)
    for m in range(M_BLK):
        pieces = []
        for e in range(PE):
            keep = jnp.where(ptgt[e] == m, 1.0, 0.0)
            pieces.append(pblk[e] * keep.astype(BF16))
        own[m * rows : (m + 1) * rows, :] = mm(jnp.concatenate(pieces, axis=1), ys)
    arrived(7)
    two = (one.astype(F32) + update(1, own[...], pw1_f, pgain, pw2_f)).astype(BF16)
    arrived(8)
    image = mm(two, dsum_w[...]).astype(BF16)
    for k in range(2):
        mall[k, me] = image[:, k * hw : (k + 1) * hw]

    def out_copy(d):
        return pltpu.make_async_remote_copy(
            mall.at[c, me], mall.at[c, me], gs_sem.at[d - 1], gr_sem.at[d - 1],
            device_id={"band": lax.rem(me + d, B)}, device_id_type=MESH,
        )

    def in_copy(d):
        src = lax.rem(me - d + B, B)
        return pltpu.make_async_remote_copy(
            mall.at[c, src], mall.at[c, src], gs_sem.at[d - 1], gr_sem.at[d - 1],
            device_id={"band": lax.rem(me + d, B)}, device_id_type=MESH,
        )

    def forward(d, half):
        src = lax.rem(me - d + B, B)
        return pltpu.make_async_remote_copy(
            mall.at[half, src], mall.at[half, src], fs_sem.at[d - 1], fr_sem.at[d - 1],
            device_id={"chan": oc}, device_id_type=MESH,
        )

    def gather_start(d, _):
        out_copy(d).start()
        return 0

    def gather_pass(d, _):
        in_copy(d).wait_recv()
        forward(d, c).start()
        return 0

    def gather_end(d, _):
        forward(d, oc).wait_recv()
        forward(d, c).wait_send()
        out_copy(d).wait_send()
        band_copy(d).wait_send()
        return 0

    lax.fori_loop(1, B, gather_start, 0, unroll=B <= 4)
    save.wait()
    to_next.wait_send()
    to_prev.wait_send()
    for cp in remote:
        cp.wait_send()
    lax.fori_loop(1, B, gather_pass, 0, unroll=B <= 4)
    lax.fori_loop(1, B, gather_end, 0, unroll=B <= 4)


def back_kernel(B, E, counts, esrc, etgt, base, mall, dblk, dgain, dw2, out, acc):
    rows = dblk.shape[1]
    hw = mall.shape[-1]
    step = pl.program_id(0)
    held = base.shape[0] // rows

    @pl.when(step == 0)
    def _():
        acc[...] = jnp.zeros_like(acc)

        def edge(e, _):
            peer = jnp.int32(0)
            end = jnp.int32(0)
            for p in range(B):
                end = end + counts[p]
                peer = peer + jnp.where(end <= e, 1, 0)
            r = pl.ds(pl.multiple_of(etgt[e] * rows, rows), rows)
            add = jnp.concatenate([mm(dblk[e], mall[k, peer, r, :]) for k in range(2)], axis=1)
            acc[esrc[e]] += add
            return 0

        lax.fori_loop(0, E, edge, 0, unroll=4)

    for i in range(held // 2):
        r = pl.ds(i * 2 * rows, 2 * rows)
        g = step * held + 2 * i
        v = base[r, :].astype(F32) + jnp.concatenate([acc[g], acc[g + 1]], axis=0)
        out[:, 0, r] = lax.dot_general(
            dw2[...], norm_silu(v, dgain[...]), (((1,), (1,)), ((), ())),
            preferred_element_type=F32,
        )


def local(
    grid_inputs, emb, counts, esrc, etgt, eblk, psrc, ptgt, pblk, bound, dblk,
    gw1, ggain, gw2, ew1, egain, ew2, pw1, pgain, pw2, dw1, dgain, dw2, B, S,
):
    E = eblk.shape[2]
    PE = pblk.shape[2]
    rows = eblk.shape[-1]
    n, ch = grid_inputs.shape[2:]
    mrows, hw = emb.shape[2:]
    lat_w = 2 * hw
    g_blk = n // rows
    smem = pl.BlockSpec(memory_space=pltpu.SMEM)
    vmem = pl.BlockSpec(memory_space=pltpu.VMEM)
    hbm = pl.BlockSpec(memory_space=pl.ANY)
    dma = pltpu.SemaphoreType.DMA
    base, mall = pl.pallas_call(
        functools.partial(front_kernel, B, S, E, PE),
        out_shape=(
            jax.ShapeDtypeStruct((n, lat_w), BF16),
            jax.ShapeDtypeStruct((2, B, mrows, hw), BF16),
        ),
        in_specs=[smem] * 6 + [vmem] * 3 + [hbm] * 11,
        out_specs=(hbm, vmem),
        scratch_shapes=[
            pltpu.VMEM((ch, n), BF16),
            pltpu.VMEM((E, rows, rows), BF16),
            pltpu.VMEM((PE, rows, rows), BF16),
            pltpu.VMEM((n, lat_w), BF16),
            pltpu.VMEM((lat_w, lat_w), BF16),
            pltpu.VMEM((mrows, lat_w), BF16),
            pltpu.VMEM((ch, lat_w), BF16),
            pltpu.VMEM((lat_w, lat_w), BF16),
            pltpu.VMEM((2, lat_w, lat_w), BF16),
            pltpu.VMEM((lat_w, lat_w), BF16),
            pltpu.VMEM((2, lat_w, lat_w), BF16),
            pltpu.VMEM((lat_w, lat_w), BF16),
            pltpu.VMEM((lat_w, lat_w), BF16),
            pltpu.VMEM((g_blk, ch, rows), BF16),
            pltpu.VMEM((E * rows, hw), BF16),
            pltpu.VMEM((mrows, hw), F32),
            pltpu.VMEM((B - 1, mrows, hw), BF16),
            pltpu.VMEM((B - 1, mrows, hw), BF16),
            pltpu.VMEM((2, mrows, hw), BF16),
            pltpu.VMEM((2, mrows, hw), BF16),
            pltpu.VMEM((2, M_BLK, rows, hw), BF16),
            pltpu.VMEM((2, rows, hw), BF16),
            pltpu.VMEM((M_BLK + 2, rows, hw), BF16),
            pltpu.VMEM((mrows, lat_w), F32),
            dma((4,)), dma((9,)), dma((9,)), dma((9,)),
            dma((B - 1,)), dma((B - 1,)),
            dma((2,)), dma((2,)), dma((2,)), dma((2,)),
            dma((B - 1,)), dma((B - 1,)), dma((B - 1,)), dma((B - 1,)),
        ],
        compiler_params=pltpu.CompilerParams(
            collective_id=0, has_side_effects=True, vmem_limit_bytes=63 * 2**20
        ),
    )(
        counts[0, 0], esrc[0, 0], etgt[0, 0], psrc[0, 0], ptgt[0, 0], bound.reshape(-1),
        ggain.reshape(1, -1), egain.reshape(1, -1), pgain.reshape(1, -1),
        grid_inputs[0, 0].T, eblk[0, 0], pblk[0, 0], emb[0, 0], gw1, gw2, ew1, ew2, pw1, pw2, dw1,
    )
    out = pl.pallas_call(
        functools.partial(back_kernel, B, E),
        out_shape=jax.ShapeDtypeStruct((ch, 1, n), F32),
        grid=(4,),
        in_specs=[smem] * 3 + [pl.BlockSpec((n // 4, lat_w), lambda i: (i, 0))] + [vmem] * 4,
        out_specs=pl.BlockSpec((ch, 1, n // 4), lambda i: (0, 0, i)),
        scratch_shapes=[pltpu.VMEM((g_blk, rows, lat_w), F32)],
        compiler_params=pltpu.CompilerParams(vmem_limit_bytes=63 * 2**20),
    )(
        counts[0, 0], esrc[0, 0], etgt[0, 0],
        base, mall, dblk[0, 0], dgain.reshape(1, -1), dw2.T,
    )
    return jnp.transpose(out, (1, 2, 0))[None]


def solution(mesh):
    B, S = mesh.shape["band"], mesh.shape["sector"]
    idx = P("band", "sector", None)
    blk = P("band", "sector", None, None, None)
    rows = P(("groups", "band"), "sector", None, None)
    w3 = P(None, None, "chan")
    w2 = P(None, "chan")
    in_specs = (
        rows, P(("groups", "band"), "sector", None, "chan"),
        idx, idx, idx, blk, idx, idx, blk, P("band", "sector", None, None), blk,
        w2, P(), w2, w3, P(), w2, w3, P(), w2, w3, P(), P(),
    )
    return jax.shard_map(
        functools.partial(local, B=B, S=S),
        mesh=mesh, in_specs=in_specs, out_specs=rows, check_vma=False,
    )
```

```python
import functools

import jax
import jax.numpy as jnp
from jax import lax
from jax.experimental import pallas as pl
from jax.experimental.pallas import tpu as pltpu
from jax.sharding import PartitionSpec as P

MESH = pl.DeviceIdType.MESH
F32 = jnp.float32
BF16 = jnp.bfloat16
M_BLK = 2


def mm(a, b):
    return jnp.dot(a, b, preferred_element_type=F32)


def norm_silu(v, gain):
    n = 1.0 / v.shape[-1]
    center = v - jnp.sum(v, axis=-1, keepdims=True) * n
    spread = jnp.sum(center * center, axis=-1, keepdims=True) * n
    half = (center * lax.rsqrt(spread + 1e-5) * (0.5 * gain)).astype(BF16)
    return half + half * jnp.tanh(half)


def front_kernel(
    B, S, E, PE,
    counts, esrc, etgt, psrc, ptgt, bound,
    ggain, egain, pgain,
    x_in, eblk_in, pblk_in, emb, gw1, gw2, ew1, ew2, pw1, pw2, dw1,
    base_out, mall,
    x, eblk, pblk, base, dsum_w,
    emb_f, gw1_f, gw2_f, ew1_f, ew2_f, pw1_f, pw2_f, dw1_f,
    xb, xs, own, psend, precv, half_send, half_recv, m1, bsend, srcs, wide,
    in_sem, loc_sem, wsend_sem, wrecv_sem, as_sem, ar_sem, hs_sem, hr_sem, bs_sem, br_sem,
    gs_sem, gr_sem, fs_sem, fr_sem,
):
    me = lax.axis_index("band")
    sec = lax.axis_index("sector")
    c = lax.axis_index("chan")
    oc = 1 - c
    hw = gw2.shape[-1]
    nxt = lax.rem(sec + 1, S)
    prv = lax.rem(sec + S - 1, S)
    mrows = emb.shape[0]
    rows = mrows // M_BLK
    cols = pl.ds(pl.multiple_of(c * hw, hw), hw)
    ocols = pl.ds(pl.multiple_of(oc * hw, hw), hw)

    parts = [
        (gw1, gw1_f.at[:, cols]),
        (gw2, gw2_f.at[:, cols]),
        (emb, emb_f.at[:, cols]),
        (ew1, ew1_f.at[:, :, cols]),
        (dw1.at[0], dw1_f.at[:, cols]),
        (ew2, ew2_f.at[:, cols]),
        (pw1, pw1_f.at[:, :, cols]),
        (pw2, pw2_f.at[:, cols]),
        (dw1.at[1], dsum_w.at[:, cols]),
    ]
    local = [pltpu.make_async_copy(s, d, loc_sem.at[i]) for i, (s, d) in enumerate(parts)]
    operands = [
        pltpu.make_async_copy(s, d, in_sem.at[i])
        for i, (s, d) in enumerate([(x_in, x), (eblk_in, eblk), (pblk_in, pblk)])
    ]
    for cp in operands[:1] + local + operands[1:]:
        cp.start()

    barrier = pltpu.get_barrier_semaphore()
    pl.semaphore_signal(barrier, inc=1, device_id={"chan": oc}, device_id_type=MESH)
    pl.semaphore_signal(barrier, inc=1, device_id={"sector": nxt}, device_id_type=MESH)
    pl.semaphore_signal(barrier, inc=1, device_id={"sector": prv}, device_id_type=MESH)
    for d in range(1, B):
        pl.semaphore_signal(
            barrier, inc=1, device_id={"band": lax.rem(me + d, B)}, device_id_type=MESH
        )
    operands[0].wait()
    for g in range(x.shape[1] // rows):
        xb[g] = x[:, g * rows : (g + 1) * rows]
    pl.semaphore_wait(barrier, B + 2)

    remote = [
        pltpu.make_async_remote_copy(
            s, d, wsend_sem.at[i], wrecv_sem.at[i], device_id={"chan": oc}, device_id_type=MESH
        )
        for i, (s, d) in enumerate(parts)
    ]
    for cp in remote:
        cp.start()

    def arrived(i):
        local[i].wait()
        remote[i].wait_recv()

    def hidden(left):
        pre = lax.dot_general(
            left, gw1_f[...], (((0,), (0,)), ((), ())), preferred_element_type=F32
        )
        return norm_silu(pre, ggain[...])

    chunk = 2 * rows
    local[1].wait()
    arrived(0)

    for e in range(0, E, 2):
        left = jnp.concatenate([xb[esrc[e]], xb[esrc[e + 1]]], axis=1)
        xs[e * rows : (e + 2) * rows, :] = mm(hidden(left), gw2_f[:, cols]).astype(BF16)

    operands[1].wait()

    def part_for(q):
        lo = jnp.int32(0)
        size = jnp.int32(0)
        for p in range(B):
            lo = lo + jnp.where(p < q, counts[p], 0)
            size = size + jnp.where(p == q, counts[p], 0)
        acc = []
        for m in range(M_BLK):
            pieces = []
            for e in range(E):
                keep = jnp.where((lo <= e) & (e < lo + size) & (etgt[e] == m), 1.0, 0.0)
                pieces.append(eblk[e] * keep.astype(BF16))
            acc.append(mm(jnp.concatenate(pieces, axis=1), xs[...]))
        return acc

    def band_copy(d):
        return pltpu.make_async_remote_copy(
            psend.at[d - 1], precv.at[d - 1], as_sem.at[d - 1], ar_sem.at[d - 1],
            device_id={"band": lax.rem(me + d, B)}, device_id_type=MESH,
        )

    def send_step(d, _):
        acc = part_for(lax.rem(me + d, B))
        for m in range(M_BLK):
            psend[d - 1, m * rows : (m + 1) * rows, :] = acc[m].astype(BF16)
        band_copy(d).start()
        return 0

    lax.fori_loop(1, B, send_step, 0, unroll=B <= 4)
    acc = part_for(me)
    for m in range(M_BLK):
        own[m * rows : (m + 1) * rows, :] = acc[m]

    arrived(2)
    arrived(3)
    wide[...] = mm(emb_f[...], ew1_f[0])
    remote[1].wait_recv()
    arrived(4)

    def base_step(i, _):
        r = pl.ds(pl.multiple_of(i * chunk, chunk), chunk)
        latent = mm(hidden(x[:, r]), gw2_f[...]).astype(BF16)
        base[r, :] = mm(latent, dw1_f[...]).astype(BF16)
        return 0

    lax.fori_loop(0, x.shape[1] // chunk, base_step, 0, unroll=2)

    save = pltpu.make_async_copy(base, base_out, in_sem.at[3])
    save.start()

    def take_step(d, _):
        band_copy(d).wait_recv()
        own[...] += precv[d - 1].astype(F32)
        return 0

    lax.fori_loop(1, B, take_step, 0, unroll=B <= 4)

    def update(k, summed, w1, gain, w2):
        half_send[k] = summed.astype(BF16)
        cp = pltpu.make_async_remote_copy(
            half_send.at[k], half_recv.at[k], hs_sem.at[k], hr_sem.at[k],
            device_id={"chan": oc}, device_id_type=MESH,
        )
        cp.start()
        pre = wide[...] + mm(half_send[k], w1[1, cols, :])
        cp.wait_recv()
        pre = pre + mm(half_recv[k], w1[1, ocols, :])
        cp.wait_send()
        return mm(norm_silu(pre, gain[...]), w2[...])

    arrived(5)
    one = (emb_f[...].astype(F32) + update(0, own[...], ew1_f, egain, ew2_f)).astype(BF16)
    for k in range(2):
        for j in range(M_BLK):
            m1[k, j] = one[j * rows : (j + 1) * rows, k * hw : (k + 1) * hw]
    bsend[0] = m1[c, bound[0]]
    bsend[1] = m1[c, bound[1]]
    to_next = pltpu.make_async_remote_copy(
        bsend.at[1], srcs.at[M_BLK], bs_sem.at[1], br_sem.at[0],
        device_id={"sector": nxt}, device_id_type=MESH,
    )
    to_prev = pltpu.make_async_remote_copy(
        bsend.at[0], srcs.at[M_BLK + 1], bs_sem.at[0], br_sem.at[1],
        device_id={"sector": prv}, device_id_type=MESH,
    )
    to_next.start()
    to_prev.start()
    for j in range(M_BLK):
        srcs[j] = m1[c, j]
    arrived(6)
    wide[...] = mm(one, pw1_f[0])
    to_next.wait_recv()
    to_prev.wait_recv()
    operands[2].wait()
    ys = jnp.concatenate([srcs[psrc[e]] for e in range(PE)], axis=0)
    for m in range(M_BLK):
        pieces = []
        for e in range(PE):
            keep = jnp.where(ptgt[e] == m, 1.0, 0.0)
            pieces.append(pblk[e] * keep.astype(BF16))
        own[m * rows : (m + 1) * rows, :] = mm(jnp.concatenate(pieces, axis=1), ys)
    arrived(7)
    two = (one.astype(F32) + update(1, own[...], pw1_f, pgain, pw2_f)).astype(BF16)
    arrived(8)
    image = mm(two, dsum_w[...]).astype(BF16)
    for k in range(2):
        mall[k, me] = image[:, k * hw : (k + 1) * hw]

    def out_copy(d):
        return pltpu.make_async_remote_copy(
            mall.at[c, me], mall.at[c, me], gs_sem.at[d - 1], gr_sem.at[d - 1],
            device_id={"band": lax.rem(me + d, B)}, device_id_type=MESH,
        )

    def in_copy(d):
        src = lax.rem(me - d + B, B)
        return pltpu.make_async_remote_copy(
            mall.at[c, src], mall.at[c, src], gs_sem.at[d - 1], gr_sem.at[d - 1],
            device_id={"band": lax.rem(me + d, B)}, device_id_type=MESH,
        )

    def forward(d, half):
        src = lax.rem(me - d + B, B)
        return pltpu.make_async_remote_copy(
            mall.at[half, src], mall.at[half, src], fs_sem.at[d - 1], fr_sem.at[d - 1],
            device_id={"chan": oc}, device_id_type=MESH,
        )

    def gather_start(d, _):
        out_copy(d).start()
        return 0

    def gather_pass(d, _):
        in_copy(d).wait_recv()
        forward(d, c).start()
        return 0

    def gather_end(d, _):
        forward(d, oc).wait_recv()
        forward(d, c).wait_send()
        out_copy(d).wait_send()
        band_copy(d).wait_send()
        return 0

    lax.fori_loop(1, B, gather_start, 0, unroll=B <= 4)
    save.wait()
    to_next.wait_send()
    to_prev.wait_send()
    for cp in remote:
        cp.wait_send()
    lax.fori_loop(1, B, gather_pass, 0, unroll=B <= 4)
    lax.fori_loop(1, B, gather_end, 0, unroll=B <= 4)


def back_kernel(B, E, counts, esrc, etgt, base, mall, dblk, dgain, dw2, out, acc):
    rows = dblk.shape[1]
    hw = mall.shape[-1]
    step = pl.program_id(0)
    held = base.shape[0] // rows

    @pl.when(step == 0)
    def _():
        acc[...] = jnp.zeros_like(acc)

        def edge(e, _):
            peer = jnp.int32(0)
            end = jnp.int32(0)
            for p in range(B):
                end = end + counts[p]
                peer = peer + jnp.where(end <= e, 1, 0)
            r = pl.ds(pl.multiple_of(etgt[e] * rows, rows), rows)
            add = jnp.concatenate([mm(dblk[e], mall[k, peer, r, :]) for k in range(2)], axis=1)
            acc[esrc[e]] += add
            return 0

        lax.fori_loop(0, E, edge, 0, unroll=4)

    for i in range(held // 2):
        r = pl.ds(i * 2 * rows, 2 * rows)
        g = step * held + 2 * i
        v = base[r, :].astype(F32) + jnp.concatenate([acc[g], acc[g + 1]], axis=0)
        out[:, 0, r] = lax.dot_general(
            dw2[...], norm_silu(v, dgain[...]), (((1,), (1,)), ((), ())),
            preferred_element_type=F32,
        )


def local(
    grid_inputs, emb, counts, esrc, etgt, eblk, psrc, ptgt, pblk, bound, dblk,
    gw1, ggain, gw2, ew1, egain, ew2, pw1, pgain, pw2, dw1, dgain, dw2, B, S,
):
    E = eblk.shape[2]
    PE = pblk.shape[2]
    rows = eblk.shape[-1]
    n, ch = grid_inputs.shape[2:]
    mrows, hw = emb.shape[2:]
    lat_w = 2 * hw
    g_blk = n // rows
    smem = pl.BlockSpec(memory_space=pltpu.SMEM)
    vmem = pl.BlockSpec(memory_space=pltpu.VMEM)
    hbm = pl.BlockSpec(memory_space=pl.ANY)
    dma = pltpu.SemaphoreType.DMA
    base, mall = pl.pallas_call(
        functools.partial(front_kernel, B, S, E, PE),
        out_shape=(
            jax.ShapeDtypeStruct((n, lat_w), BF16),
            jax.ShapeDtypeStruct((2, B, mrows, hw), BF16),
        ),
        in_specs=[smem] * 6 + [vmem] * 3 + [hbm] * 11,
        out_specs=(hbm, vmem),
        scratch_shapes=[
            pltpu.VMEM((ch, n), BF16),
            pltpu.VMEM((E, rows, rows), BF16),
            pltpu.VMEM((PE, rows, rows), BF16),
            pltpu.VMEM((n, lat_w), BF16),
            pltpu.VMEM((lat_w, lat_w), BF16),
            pltpu.VMEM((mrows, lat_w), BF16),
            pltpu.VMEM((ch, lat_w), BF16),
            pltpu.VMEM((lat_w, lat_w), BF16),
            pltpu.VMEM((2, lat_w, lat_w), BF16),
            pltpu.VMEM((lat_w, lat_w), BF16),
            pltpu.VMEM((2, lat_w, lat_w), BF16),
            pltpu.VMEM((lat_w, lat_w), BF16),
            pltpu.VMEM((lat_w, lat_w), BF16),
            pltpu.VMEM((g_blk, ch, rows), BF16),
            pltpu.VMEM((E * rows, hw), BF16),
            pltpu.VMEM((mrows, hw), F32),
            pltpu.VMEM((B - 1, mrows, hw), BF16),
            pltpu.VMEM((B - 1, mrows, hw), BF16),
            pltpu.VMEM((2, mrows, hw), BF16),
            pltpu.VMEM((2, mrows, hw), BF16),
            pltpu.VMEM((2, M_BLK, rows, hw), BF16),
            pltpu.VMEM((2, rows, hw), BF16),
            pltpu.VMEM((M_BLK + 2, rows, hw), BF16),
            pltpu.VMEM((mrows, lat_w), F32),
            dma((4,)), dma((9,)), dma((9,)), dma((9,)),
            dma((B - 1,)), dma((B - 1,)),
            dma((2,)), dma((2,)), dma((2,)), dma((2,)),
            dma((B - 1,)), dma((B - 1,)), dma((B - 1,)), dma((B - 1,)),
        ],
        compiler_params=pltpu.CompilerParams(
            collective_id=0, has_side_effects=True, vmem_limit_bytes=63 * 2**20
        ),
    )(
        counts[0, 0], esrc[0, 0], etgt[0, 0], psrc[0, 0], ptgt[0, 0], bound.reshape(-1),
        ggain.reshape(1, -1), egain.reshape(1, -1), pgain.reshape(1, -1),
        grid_inputs[0, 0].T, eblk[0, 0], pblk[0, 0], emb[0, 0], gw1, gw2, ew1, ew2, pw1, pw2, dw1,
    )
    out = pl.pallas_call(
        functools.partial(back_kernel, B, E),
        out_shape=jax.ShapeDtypeStruct((ch, 1, n), F32),
        grid=(4,),
        in_specs=[smem] * 3 + [pl.BlockSpec((n // 4, lat_w), lambda i: (i, 0))] + [vmem] * 4,
        out_specs=pl.BlockSpec((ch, 1, n // 4), lambda i: (0, 0, i)),
        scratch_shapes=[pltpu.VMEM((g_blk, rows, lat_w), F32)],
        compiler_params=pltpu.CompilerParams(vmem_limit_bytes=63 * 2**20),
    )(
        counts[0, 0], esrc[0, 0], etgt[0, 0],
        base, mall, dblk[0, 0], dgain.reshape(1, -1), dw2.T,
    )
    return jnp.transpose(out, (1, 2, 0))[None]


def solution(mesh):
    B, S = mesh.shape["band"], mesh.shape["sector"]
    idx = P("band", "sector", None)
    blk = P("band", "sector", None, None, None)
    rows = P(("groups", "band"), "sector", None, None)
    w3 = P(None, None, "chan")
    w2 = P(None, "chan")
    in_specs = (
        rows, P(("groups", "band"), "sector", None, "chan"),
        idx, idx, idx, blk, idx, idx, blk, P("band", "sector", None, None), blk,
        w2, P(), w2, w3, P(), w2, w3, P(), w2, w3, P(), P(),
    )
    return jax.shard_map(
        functools.partial(local, B=B, S=S),
        mesh=mesh, in_specs=in_specs, out_specs=rows, check_vma=False,
    )
```
